256 devices in a mesh: ctx: 8 (over y, x_hi), exp: 32 (over z, x_lo, core).
Axes of the slice: x: 4 (x_hi: 2, x_lo: 2; x = x_hi * 2 + x_lo), y: 4, z: 8, core: 2. Of those that a mesh axis runs over, the one named last changes fastest.
Arguments:
- queries: bfloat16 [2048, 8192], P('ctx', 'exp'), may hold values from -10 to 10
- keys: bfloat16 [16384, 512], P('ctx'), may hold values from -10 to 10
- values: bfloat16 [16384, 512], P('ctx'), may hold values from -6 to 6
- block_offsets: int32 [8], replicated, may hold values from 0 to 1792
- w_out: bfloat16 [8192, 4096], P('exp'), may hold values from -0.0625 to 0.0625
- residual: bfloat16 [2048, 4096], P(('ctx', 'exp')), may hold values from -40 to 40
- norm_gain: float32 [4096], replicated, may hold values from 0.1 to 1.9
- expert_ids: int32 [8, 256, 8], P(None, 'exp'), may hold values from 0 to 63, all different within a row; in each aligned block of 8 rows (0 to 7, 8 to 15, ..., all dimensions but the last counted through in order) at most 2 rows name the same one
- gate_weights: float32 [8, 256, 8], P(None, 'exp'), may hold values from 0.05 to 0.3
- w_gate: bfloat16 [64, 4096, 1024], P('exp', None, 'ctx'), may hold values from -0.09375 to 0.09375
- w_up: bfloat16 [64, 4096, 1024], P('exp', None, 'ctx'), may hold values from -0.09375 to 0.09375
- w_down: bfloat16 [64, 1024, 4096], P('exp', 'ctx'), may hold values from -0.1875 to 0.1875
Outputs:
- attended: bfloat16 [2048, 4096], P(('ctx', 'exp'))
- expert_mix: bfloat16 [2048, 4096], P(('ctx', 'exp'))
The draws below stay inside these ranges and needn't reach their ends.
Inputs may be any that keep to these rules, and one draw needn't show every extreme that they name: `expert_ids`: each row names 8 different experts. Among the 8 rows of one device (aligned blocks of rows of the first two dimensions taken together), no expert is named more than 2 times, and in every draw some expert is named exactly 2 times there.
All inputs are finite; a program needn't handle non-finite values.
Results may differ from the reference program's by a relative error of at most 0.03.
Values may be sent and summed in bfloat16 or wider, within the bound.
No kernel may reach another device: no remote copies, remote signals or barrier semaphores. Data moves between devices by JAX's collectives and lax.ppermute only.
A program may use at most 128 MiB of HBM per device.

```python
import math
import jax
import jax.numpy as jnp
import numpy as np
from jax import lax

MODEL_DIM = 4096
Q_HEADS = 64
KV_HEADS = 4
HEAD_DIM = 128
EXPERT_FF = 1024
TOP_K = 8
KEYS_DEV = 2048
QUERY_BLOCK = 256
EXPERTS = 64
SEQUENCE = 16384
TOKENS = 2048
ROWS_DEV = 8
CAPACITY = 2
GROUP_SIZE = 16
HIDDEN_SLICE = 128
N_CTX = 8
N_EXP = 32


def draw_queries(key, part):
    key = jax.random.fold_in(key, 11)
    layout = (TOKENS, Q_HEADS * HEAD_DIM)
    return jnp.clip(jax.random.normal(key, layout, jnp.float32), -6.0, 6.0).astype(jnp.bfloat16)


def draw_keys(key, part):
    key = jax.random.fold_in(key, 12)
    layout = (SEQUENCE, KV_HEADS * HEAD_DIM)
    return jnp.clip(2.5 * jax.random.normal(key, layout, jnp.float32), -10.0, 10.0).astype(jnp.bfloat16)


def draw_residual(key, part):
    key = jax.random.fold_in(key, 13)
    column_key, row_key, noise_key = jax.random.split(key, 3)
    column_scale = jnp.exp(jax.random.uniform(column_key, (MODEL_DIM,), jnp.float32, 0.0, math.log(10.0)))
    row_scale = jnp.exp(jax.random.uniform(row_key, (TOKENS,), jnp.float32, 0.0, math.log(10.0)))
    noise = jnp.clip(jax.random.normal(noise_key, (TOKENS, MODEL_DIM), jnp.float32), -4.0, 4.0)
    return (0.1 * noise * column_scale[None, :] * row_scale[:, None]).astype(jnp.bfloat16)


def touch_ends(entries, rng, smallest, top_value):
    longest = entries.shape.index(max(entries.shape))
    spots = []
    for shift in (0, 1):
        where = [jax.random.randint(jax.random.fold_in(rng, axis), (), 0, length) for axis, length in enumerate(entries.shape)]
        where[longest] = (where[longest] + shift) % entries.shape[longest]
        spots.append(tuple(where))
    return entries.at[spots[0]].set(smallest).at[spots[1]].set(top_value)


def block_levels(own_key, extent, shards, least, high):
    factor_of = 1.0
    for axis_at, blocks in shards:
        draws = jax.random.uniform(jax.random.fold_in(jax.random.fold_in(own_key, 6), axis_at), (blocks,), jnp.float32, least / len(shards), high / len(shards))
        factor_of = factor_of * jnp.repeat(jnp.exp(draws), extent[axis_at] // blocks).reshape((-1,) + (1,) * (len(extent) - 1 - axis_at))
    return factor_of


def deal_out(own_key, own, number, rows, number_of, top, reach, lean):
    ranking = jax.random.permutation(own_key, number_of)
    heavy_load, usual = shares(number_of, rows * top, reach, lean, True), shares(number_of, rows * top, reach, lean, False)
    places = jnp.arange(number_of)

    def named(lengths, rotation):
        used = int((lengths > 0).sum())
        fixed = max(1, used // 4)
        moved = fixed + (places - fixed + rotation * (used - fixed)) % max(1, number_of - fixed)
        return jnp.zeros((number_of,), jnp.int32).at[ranking[jnp.where(places < fixed, places, moved)]].set(jnp.asarray(lengths, jnp.int32))

    lengths = jnp.where(number % 4 == 0, named(heavy_load, number // 4), named(usual, number - number // 4 - 1))
    mixed = jax.random.permutation(jax.random.fold_in(own, 3), number_of)
    giver, sink = mixed[0:number_of // 2 * 2:2], mixed[1:number_of // 2 * 2:2]
    margin = jnp.minimum(lengths[giver] - 1, reach - lengths[sink]) // 2
    margin = jnp.where((giver == ranking[0]) | (sink == ranking[0]) | (lengths[sink] == 0), 0, jnp.maximum(margin, 0))
    moved = jax.random.randint(jax.random.fold_in(own, 4), (number_of // 2,), 0, 1 << 20) % (margin + 1)
    lengths = lengths.at[giver].add(-moved).at[sink].add(moved)
    items = jnp.searchsorted(jnp.cumsum(lengths), jnp.arange(rows * top), side="right").astype(jnp.int32)
    listing = items.reshape(top, rows).T
    listing = listing[jax.random.permutation(jax.random.fold_in(own, 1), rows)]
    rotation = jax.random.randint(jax.random.fold_in(own, 2), (rows, 1), 0, top)
    return jnp.take_along_axis(listing, (jnp.arange(top)[None, :] + rotation) % top, axis=1)


def shares(count, total, most, skew, full):
    portions = [(1 << 20) // math.isqrt(standing ** skew) + 1 for standing in range(1, count + 1)]
    largest = most if full else min(most, max(-(-total // count), total * portions[0] // sum(portions)))
    least = 1 if total - largest >= count - 1 else 0
    given, spare = [largest] + [least] * (count - 1), total - largest - least * (count - 1)
    while spare > 0:
        movable = [i for i in range(1, count) if given[i] < largest] or [i for i in range(1, count) if given[i] < most]
        mass, remaining = sum([portions[i] for i in movable]), spare
        for i in movable:
            extra = min(most - given[i], max(1, remaining * portions[i] // mass), spare)
            given[i] = given[i] + extra
            spare = spare - extra
    return np.array(given)


def gaussian(stream_key, extent, deviation, most, pieces=(), held_as=jnp.bfloat16):
    drawn = deviation * jax.random.normal(stream_key, extent, jnp.float32)
    if pieces:
        drawn = drawn * block_levels(stream_key, extent, pieces, -0.22, 0.18)
    return jnp.clip(drawn, -most, most).astype(held_as)


def setup_inputs(seed: int = 0) -> dict:
    seeds = jax.random.split(jax.random.key(seed), 13)
    queries = draw_queries(jax.random.fold_in(seeds[12], 71), 0)
    keys = draw_keys(jax.random.fold_in(seeds[12], 71), 0)
    values = gaussian(seeds[2], (SEQUENCE, KV_HEADS * HEAD_DIM), 1.0, 6.0, ((0, 8),))
    block_offsets = touch_ends(jax.random.randint(seeds[3], (N_CTX,), 0, KEYS_DEV - QUERY_BLOCK + 1), jax.random.fold_in(seeds[3], 1), 0, KEYS_DEV - QUERY_BLOCK).astype(jnp.int32)
    w_out = gaussian(seeds[4], (Q_HEADS * HEAD_DIM, MODEL_DIM), (Q_HEADS * HEAD_DIM) ** -0.5, 0.0625, ((0, 32),))
    residual = draw_residual(jax.random.fold_in(seeds[12], 71), 0)
    norm_gain = jnp.clip(1.0 + 0.18 * jax.random.normal(seeds[6], (MODEL_DIM,), jnp.float32), 0.1, 1.9)
    expert_ids_keys = jax.random.split(jax.random.fold_in(seeds[7], 1), N_CTX * QUERY_BLOCK // ROWS_DEV)
    expert_ids_turns = jax.random.permutation(jax.random.fold_in(seeds[7], 3), N_CTX * QUERY_BLOCK // ROWS_DEV)
    expert_ids = jax.vmap(lambda own, number: deal_out(jax.random.fold_in(seeds[7], 2), own, number, ROWS_DEV, EXPERTS, TOP_K, CAPACITY, 2))(expert_ids_keys, expert_ids_turns).reshape((N_CTX, QUERY_BLOCK, TOP_K))
    gate_weights = jnp.clip(0.05 + 0.25 * jax.random.uniform(seeds[8], (N_CTX, QUERY_BLOCK, TOP_K), jnp.float32) ** block_levels(seeds[8], (N_CTX, QUERY_BLOCK, TOP_K), ((1, 32),), -0.2, 0.2), 0.05, 0.3)
    w_gate = gaussian(seeds[9], (EXPERTS, MODEL_DIM, EXPERT_FF), MODEL_DIM ** -0.5, 0.09375, ((0, 32), (2, 8)))
    w_up = gaussian(seeds[10], (EXPERTS, MODEL_DIM, EXPERT_FF), MODEL_DIM ** -0.5, 0.09375, ((0, 32), (2, 8)))
    w_down = gaussian(seeds[11], (EXPERTS, EXPERT_FF, MODEL_DIM), EXPERT_FF ** -0.5, 0.1875, ((0, 32), (1, 8)))
    return dict(queries=queries, keys=keys, values=values, block_offsets=block_offsets, w_out=w_out, residual=residual, norm_gain=norm_gain, expert_ids=expert_ids, gate_weights=gate_weights, w_gate=w_gate, w_up=w_up, w_down=w_down)


def reference(queries, keys, values, block_offsets, w_out, residual, norm_gain, expert_ids, gate_weights, w_gate, w_up, w_down):
    owner_block = jnp.arange(TOKENS, dtype=jnp.int32) // QUERY_BLOCK
    within = jnp.arange(TOKENS, dtype=jnp.int32) % QUERY_BLOCK
    query_pos = owner_block * KEYS_DEV + block_offsets[owner_block] + within
    key_pos = jnp.arange(SEQUENCE, dtype=jnp.int32)
    visible = key_pos[None, :] <= query_pos[:, None]
    inverse_root = 1.0 / math.sqrt(HEAD_DIM)
    query_heads = queries.reshape(TOKENS, Q_HEADS, HEAD_DIM).transpose(1, 0, 2)
    key_heads = keys.reshape(SEQUENCE, KV_HEADS, HEAD_DIM).transpose(1, 0, 2)
    value_heads = values.reshape(SEQUENCE, KV_HEADS, HEAD_DIM).transpose(1, 0, 2)

    def one_head(head):
        query_rows = query_heads[head]
        key_rows = key_heads[head // GROUP_SIZE]
        value_rows = value_heads[head // GROUP_SIZE]
        scores = jnp.dot(query_rows, key_rows.T, preferred_element_type=jnp.float32) * inverse_root
        scores = jnp.where(visible, scores, -1e+30)
        highest = lax.optimization_barrier(jnp.max(scores, axis=1, keepdims=True))
        probabilities = jnp.where(visible, jnp.exp(scores - highest), 0.0)
        denominators = lax.optimization_barrier(jnp.sum(probabilities, axis=1, keepdims=True))
        rounded_probs = probabilities.astype(jnp.bfloat16)
        mixed = jnp.dot(rounded_probs, value_rows, preferred_element_type=jnp.float32) / denominators
        return mixed.astype(jnp.bfloat16)
    head_outputs = lax.map(one_head, jnp.arange(Q_HEADS, dtype=jnp.int32))
    attention = head_outputs.transpose(1, 0, 2).reshape(TOKENS, Q_HEADS * HEAD_DIM)
    attended = jnp.dot(attention, w_out, preferred_element_type=jnp.float32).astype(jnp.bfloat16)
    hidden = residual.astype(jnp.float32) + lax.optimization_barrier(attended).astype(jnp.float32)
    normed = (hidden * lax.rsqrt(lax.optimization_barrier(jnp.mean(hidden * hidden, axis=1, keepdims=True)) + 1e-06) * norm_gain).astype(jnp.bfloat16)
    chosen_ids = expert_ids.reshape(TOKENS, TOP_K)
    chosen_weights = gate_weights.reshape(TOKENS, TOP_K)
    limit = N_CTX * N_EXP * CAPACITY

    def one_expert(running, expert):
        matches = chosen_ids == expert
        weight_of = lax.optimization_barrier(jnp.sum(jnp.where(matches, chosen_weights, 0.0), axis=1))
        picked = jnp.any(matches, axis=1)
        picked_count = jnp.sum(picked.astype(jnp.int32))
        row_index = jnp.nonzero(picked, size=limit, fill_value=0)[0].astype(jnp.int32)
        tokens_in = normed[row_index]
        gate_out = jnp.dot(tokens_in, w_gate[expert], preferred_element_type=jnp.float32)
        up_out = jnp.dot(tokens_in, w_up[expert], preferred_element_type=jnp.float32)
        activated = (jax.nn.silu(gate_out) * up_out).astype(jnp.bfloat16)
        grouped = activated.reshape(limit, N_CTX, HIDDEN_SLICE).astype(jnp.float32)
        down_groups = w_down[expert].reshape(N_CTX, HIDDEN_SLICE, MODEL_DIM).astype(jnp.float32)
        group_terms = jnp.einsum('rcf,cfd->rcd', grouped, down_groups, precision=lax.Precision.HIGHEST).astype(jnp.bfloat16)
        expert_out = lax.optimization_barrier(jnp.sum(group_terms.astype(jnp.float32), axis=1))
        row_weight = jnp.where(jnp.arange(limit, dtype=jnp.int32) < picked_count, weight_of[row_index], 0.0)
        running = running.at[row_index].add(row_weight[:, None] * expert_out)
        return (running, None)
    start_sum = jnp.zeros((TOKENS, MODEL_DIM), jnp.float32)
    mixture, _ = lax.scan(one_expert, start_sum, jnp.arange(EXPERTS, dtype=jnp.int32))
    return (attended, mixture.astype(jnp.bfloat16))
```

```python
import functools
import math

import jax
import jax.numpy as jnp
from jax import lax
from jax.experimental import pallas as pl
from jax.experimental.pallas import tpu as pltpu
from jax.sharding import PartitionSpec as P

Q_HEADS = 64
KV_HEADS = 4
HEAD_DIM = 128

NY, NXH, NZ, NXL, NC = 4, 2, 8, 2, 2
NX = NXH * NXL
CTX = NY * NXH
CHIPS_EXP = NZ * NXL
AXES = ("ctx", "exp")

LOWEST = -1e30
SCALE = 1.0 / math.sqrt(HEAD_DIM)
SCALE2 = SCALE * math.log2(math.e)

COLS_A = 1792
GATE_COLS = 128
SPLIT = COLS_A + GATE_COLS

STAT_ROWS = 16
KEY_CHUNK = 256


def linear(y, x, z, core):
    ctx = (y % NY) * NXH + (x % NX) // NXL
    exp = (z % NZ) * NXL * NC + (x % NXL) * NC + core % NC
    return ctx * (NZ * NXL * NC) + exp


def moved(array, dy=0, dx=0, dz=0, dcore=0):
    pairs = [
        (linear(y, x, z, c), linear(y + dy, x + dx, z + dz, c + dcore))
        for y in range(NY)
        for x in range(NX)
        for z in range(NZ)
        for c in range(NC)
    ]
    return lax.ppermute(array, AXES, pairs)


def same_core_groups():
    return [[i * NC + c for i in range(CHIPS_EXP)] for c in range(NC)]


def partial_attention(place, q_ref, k_ref, v_ref, out_ref, vt_ref, s_ref, p_ref):
    source = pl.program_id(0)
    own = place[1]
    rows = q_ref.shape[1]
    keys = k_ref.shape[0]

    @pl.when(source == 0)
    def _():
        vt_ref[...] = v_ref[...].T

    def unit(masked):
        stats = []
        for head in range(2):
            query = q_ref[0, :, head * HEAD_DIM : (head + 1) * HEAD_DIM]
            top = jnp.full((8, rows), LOWEST, jnp.float32)
            for start in range(0, keys, KEY_CHUNK):
                part = lax.dot_general(
                    k_ref[start : start + KEY_CHUNK, :],
                    query,
                    (((1,), (1,)), ((), ())),
                    preferred_element_type=jnp.float32,
                )
                if masked:
                    key_at = start + lax.broadcasted_iota(jnp.int32, part.shape, 0)
                    row_at = place[2] + lax.broadcasted_iota(jnp.int32, part.shape, 1)
                    part = jnp.where(key_at <= row_at, part, LOWEST)
                s_ref[head, start : start + KEY_CHUNK, :] = part
                top = jnp.maximum(top, jnp.max(part.reshape(-1, 8, rows), axis=0))
            highest = jnp.max(top, axis=0, keepdims=True) * SCALE2
            total = jnp.zeros((8, rows), jnp.float32)
            for start in range(0, keys, KEY_CHUNK):
                weights = jnp.exp2(s_ref[head, start : start + KEY_CHUNK, :] * SCALE2 - highest)
                total = total + jnp.sum(weights.reshape(-1, 8, rows), axis=0)
                p_ref[head, start : start + KEY_CHUNK, :] = weights.astype(jnp.bfloat16)
            weight_sum = jnp.sum(total, axis=0, keepdims=True)
            mixed = jnp.dot(vt_ref[...], p_ref[head], preferred_element_type=jnp.float32)
            out_ref[0, head * HEAD_DIM : (head + 1) * HEAD_DIM, :] = (mixed / weight_sum).astype(
                jnp.bfloat16
            )
            stats.append(highest + jnp.log2(weight_sum))
        write_stats(stats)

    def write_stats(stats):
        pieces = []
        for stat in stats:
            high = stat.astype(jnp.bfloat16).astype(jnp.float32)
            middle = (stat - high).astype(jnp.bfloat16).astype(jnp.float32)
            pieces += [high, middle, stat - high - middle]
        pieces.append(jnp.zeros((STAT_ROWS - len(pieces), rows), jnp.float32))
        out_ref[0, 2 * HEAD_DIM :, :] = jnp.concatenate(pieces, axis=0).astype(jnp.bfloat16)

    @pl.when(source > own)
    def _():
        unit(False)

    @pl.when(source == own)
    def _():
        unit(True)

    @pl.when(source < own)
    def _():
        out_ref[0, : 2 * HEAD_DIM, :] = jnp.zeros((2 * HEAD_DIM, rows), jnp.bfloat16)
        write_stats([jnp.full((1, rows), LOWEST, jnp.float32)] * 2)


def attend(place, all_queries, keys, values):
    sources, rows, width = all_queries.shape
    keys_dev = keys.shape[0]
    out_rows = 2 * HEAD_DIM + STAT_ROWS
    return pl.pallas_call(
        partial_attention,
        out_shape=jax.ShapeDtypeStruct((sources, out_rows, rows), jnp.bfloat16),
        grid_spec=pltpu.PrefetchScalarGridSpec(
            num_scalar_prefetch=1,
            grid=(sources,),
            in_specs=[
                pl.BlockSpec((1, rows, width), lambda i, place: (i, 0, 0)),
                pl.BlockSpec((keys_dev, HEAD_DIM), lambda i, place: (0, place[0])),
                pl.BlockSpec((keys_dev, HEAD_DIM), lambda i, place: (0, place[0])),
            ],
            out_specs=pl.BlockSpec((1, out_rows, rows), lambda i, place: (i, 0, 0)),
            scratch_shapes=[
                pltpu.VMEM((HEAD_DIM, keys_dev), jnp.bfloat16),
                pltpu.VMEM((2, keys_dev, rows), jnp.float32),
                pltpu.VMEM((2, keys_dev, rows), jnp.bfloat16),
            ],
        ),
        compiler_params=pltpu.CompilerParams(vmem_limit_bytes=40 * 1024 * 1024),
    )(place, all_queries, keys, values)


def combine(partials):
    shards, _, rows = partials.shape
    mixed = partials[:, : 2 * HEAD_DIM].astype(jnp.float32).reshape(shards, 2, HEAD_DIM, rows)
    stats = partials[:, 2 * HEAD_DIM : 2 * HEAD_DIM + 6].astype(jnp.float32).reshape(shards, 2, 3, rows)
    levels = jnp.sum(stats, axis=2)
    shares = jnp.exp2(levels - jnp.max(levels, axis=0, keepdims=True))
    shares = shares / jnp.sum(shares, axis=0, keepdims=True)
    return jnp.sum(mixed * shares[:, :, None, :], axis=0).astype(jnp.bfloat16).reshape(-1, rows)


def gather_direct(block, axis):
    return [block] + [moved(block, **{axis: step}) for step in (1, -1, 2)]


def gather_ring(block, axis, size):
    half = size // 2
    found = {0: block}
    up = down = block
    for step in range(1, half):
        up = moved(up, **{axis: 1})
        down = moved(down, **{axis: -1})
        found[step] = up
        found[size - step] = down
    cut = block.shape[0] // 2
    first = moved(up[:cut], **{axis: 1})
    second = moved(down[cut:], **{axis: -1})
    found[half] = jnp.concatenate([first, second], axis=0)
    return [found[r] for r in range(size)]


def add(a, b):
    return (a.astype(jnp.float32) + b.astype(jnp.float32)).astype(jnp.bfloat16)


def reduce_ring(blocks, axis):
    size = len(blocks)
    half = size // 2
    cut = blocks[half].shape[0] // 2
    down = moved(blocks[half][:cut], **{axis: -1})
    up = moved(blocks[half][cut:], **{axis: 1})
    at = blocks[half - 1]
    down = jnp.concatenate([add(at[:cut], down), at[cut:]], axis=0)
    at = blocks[half + 1]
    up = jnp.concatenate([at[:cut], add(at[cut:], up)], axis=0)
    for step in range(half - 2, 0, -1):
        down = add(moved(down, **{axis: -1}), blocks[step])
        up = add(moved(up, **{axis: 1}), blocks[size - step])
    down = moved(down, **{axis: -1})
    up = moved(up, **{axis: 1})
    return (
        blocks[0].astype(jnp.float32) + down.astype(jnp.float32) + up.astype(jnp.float32)
    ).astype(jnp.bfloat16)


def reduce_direct(block, axis):
    own, near, far, across = jnp.split(block, 4, axis=0)
    terms = [
        own,
        moved(near, **{axis: -1}),
        moved(far, **{axis: 1}),
        moved(across, **{axis: -2}),
    ]
    return sum(t.astype(jnp.float32) for t in terms)


def gate_columns(ids, weights, experts):
    matches = ids[:, :, None] == jnp.arange(experts, dtype=jnp.int32)[None, None, :]
    dense = jnp.sum(jnp.where(matches, weights[:, :, None], 0.0), axis=1)
    high = dense.astype(jnp.bfloat16)
    low = (dense - high.astype(jnp.float32)).astype(jnp.bfloat16)
    return jnp.concatenate([high, low], axis=1)


def on_device(
    queries,
    keys,
    values,
    block_offsets,
    w_out,
    residual,
    norm_gain,
    expert_ids,
    gate_weights,
    w_gate,
    w_up,
    w_down,
):
    ctx_pos = lax.axis_index("ctx")
    exp_pos = lax.axis_index("exp")
    core = exp_pos % NC
    block_len, query_width = queries.shape
    model_width = residual.shape[1]
    half_width = model_width // 2
    heads_here = query_width // HEAD_DIM
    key_head = exp_pos * heads_here // (Q_HEADS // KV_HEADS)

    local_experts, _, hidden = w_gate.shape
    experts = local_experts * lax.axis_size("exp")
    own_in = jnp.concatenate([w_gate[0], w_gate[1], w_up[0], w_up[1]], axis=1)
    own_down = w_down.reshape(local_experts * hidden, model_width)
    own_out = lax.dynamic_slice_in_dim(w_out, core * half_width, half_width, 1)
    give_out = lax.dynamic_slice_in_dim(w_out, (1 - core) * half_width, half_width, 1)
    other_out = moved(give_out, dcore=1)
    other_in = moved(own_in, dcore=1)
    other_down = moved(own_down, dcore=1)

    place = jnp.stack([key_head, ctx_pos, block_offsets[ctx_pos]]).astype(jnp.int32)
    copies = lax.optimization_barrier(
        jnp.broadcast_to(queries[None], (CTX, block_len, query_width))
    )
    all_queries = lax.all_to_all(copies, "ctx", split_axis=0, concat_axis=0, tiled=True)
    partials = attend(place, all_queries, keys, values)
    partials = lax.all_to_all(partials, "ctx", split_axis=0, concat_axis=0, tiled=True)
    own_att = combine(partials)
    other_att = moved(own_att, dcore=1)

    contract = (((0,), (0,)), ((), ()))
    projected = lax.dot_general(
        own_att, own_out, contract, preferred_element_type=jnp.float32
    ) + lax.dot_general(other_att, other_out, contract, preferred_element_type=jnp.float32)
    chip_rows = block_len // CHIPS_EXP
    rows_dev = chip_rows // NC
    terms = projected.astype(jnp.bfloat16).reshape(CHIPS_EXP, chip_rows, half_width)
    terms = lax.all_to_all(
        terms, "exp", split_axis=0, concat_axis=0, tiled=True, axis_index_groups=same_core_groups()
    )
    att_half = jnp.sum(terms.astype(jnp.float32), axis=0).astype(jnp.bfloat16)
    keep = lax.dynamic_slice_in_dim(att_half, core * rows_dev, rows_dev, 0)
    give = lax.dynamic_slice_in_dim(att_half, (1 - core) * rows_dev, rows_dev, 0)
    came = moved(give, dcore=1)
    attended = jnp.where(
        core == 0,
        jnp.concatenate([keep, came], axis=1),
        jnp.concatenate([came, keep], axis=1),
    )

    hidden_rows = residual.astype(jnp.float32) + attended.astype(jnp.float32)
    normed = (
        hidden_rows
        * lax.rsqrt(jnp.mean(hidden_rows * hidden_rows, axis=1, keepdims=True) + 1e-06)
        * norm_gain
    ).astype(jnp.bfloat16)

    gates = gate_columns(expert_ids[ctx_pos], gate_weights[ctx_pos], experts)
    row = jnp.concatenate([normed[:, :COLS_A], gates, normed[:, COLS_A:]], axis=1)
    line = jnp.concatenate(gather_direct(row, "dx"), axis=0)
    part_a, part_b = line[:, :SPLIT], line[:, SPLIT:]
    line_rows = line.shape[0]
    sheet_a = jnp.concatenate(gather_direct(part_a, "dy"), axis=0)
    sheet_b = jnp.concatenate(gather_ring(part_b, "dz", NZ), axis=0)
    chunks_a = gather_ring(sheet_a, "dz", NZ)
    chunks_b = gather_ring(sheet_b, "dy", NY)
    order = (0, 1, 3, 2)

    first_expert = (exp_pos // NC) * NC * local_experts
    hidden_all = local_experts * hidden
    column = jnp.arange(hidden_all, dtype=jnp.int32) // hidden
    gate_row = jnp.arange(GATE_COLS, dtype=jnp.int32) % experts
    own_pick = (gate_row[:, None] == (first_expert + core * local_experts + column)[None, :]).astype(
        jnp.bfloat16
    )
    other_pick = (
        gate_row[:, None] == (first_expert + (1 - core) * local_experts + column)[None, :]
    ).astype(jnp.bfloat16)

    def f32dot(a, b):
        return jnp.dot(a, b, preferred_element_type=jnp.float32)

    acts_by_side = []
    for w_in, pick in ((own_in, own_pick), (other_in, other_pick)):
        from_a = [f32dot(c[:, :COLS_A], w_in[:COLS_A]) for c in chunks_a]
        factors = [f32dot(c[:, COLS_A:], pick) for c in chunks_a]
        from_b = [f32dot(c, w_in[COLS_A:]) for c in chunks_b]
        acts = []
        for at, distance in enumerate(order):
            rows = slice(at * line_rows, (at + 1) * line_rows)
            both = from_b[distance] + jnp.concatenate([p[rows] for p in from_a], axis=0)
            factor = jnp.concatenate([p[rows] for p in factors], axis=0)
            gate, up = both[:, :hidden_all], both[:, hidden_all:]
            acts.append((gate / (1.0 + jnp.exp(-gate)) * up * factor).astype(jnp.bfloat16))
        acts_by_side.append(acts)

    own_acts, other_acts = acts_by_side

    def down(own, other, columns):
        return (f32dot(own, own_down[:, columns]) + f32dot(other, other_down[:, columns])).astype(
            jnp.bfloat16
        )

    terms_a = []
    for r in range(NZ):
        rows = slice(r * line_rows, (r + 1) * line_rows)
        terms_a.append(
            down(
                jnp.concatenate([a[rows] for a in own_acts], axis=0),
                jnp.concatenate([a[rows] for a in other_acts], axis=0),
                slice(0, COLS_A),
            )
        )
    terms_b = [None] * NY
    for at, distance in enumerate(order):
        terms_b[distance] = down(own_acts[at], other_acts[at], slice(COLS_A, None))

    sum_a = reduce_ring(terms_a, "dz")
    sum_b = reduce_ring(terms_b, "dy")
    line_a = reduce_direct(sum_a, "dy").astype(jnp.bfloat16)
    line_b = reduce_ring(jnp.split(sum_b, NZ, axis=0), "dz")
    mixture = reduce_direct(jnp.concatenate([line_a, line_b], axis=1), "dx")
    return (attended, mixture.astype(jnp.bfloat16))


def solution(mesh):
    in_specs = (
        P("ctx", "exp"),
        P("ctx", None),
        P("ctx", None),
        P(),
        P("exp", None),
        P(("ctx", "exp"), None),
        P(),
        P(None, "exp", None),
        P(None, "exp", None),
        P("exp", None, "ctx"),
        P("exp", None, "ctx"),
        P("exp", "ctx", None),
    )
    out_specs = (P(("ctx", "exp"), None), P(("ctx", "exp"), None))
    return jax.shard_map(
        on_device, mesh=mesh, in_specs=in_specs, out_specs=out_specs, check_vma=False
    )
```

```python
import functools
import math

import jax
import jax.numpy as jnp
from jax import lax
from jax.experimental import pallas as pl
from jax.experimental.pallas import tpu as pltpu
from jax.sharding import PartitionSpec as P

Q_HEADS = 64
KV_HEADS = 4
HEAD_DIM = 128

NY, NXH, NZ, NXL, NC = 4, 2, 8, 2, 2
NX = NXH * NXL
CTX = NY * NXH
CHIPS_EXP = NZ * NXL
AXES = ("ctx", "exp")

LOWEST = -1e30
SCALE = 1.0 / math.sqrt(HEAD_DIM)
SCALE2 = SCALE * math.log2(math.e)

COLS_A = 2048
GATE_COLS = 128
SPLIT = COLS_A + GATE_COLS

STAT_ROWS = 16
HALF_ROWS = 16
KEY_CHUNK = 256
VMEM_LIMIT = 56 * 1024 * 1024
UP_ROWS = 512
DOWN_ROWS = 512
DOWN_COLS = 512


def linear(y, x, z, core):
    ctx = (y % NY) * NXH + (x % NX) // NXL
    exp = (z % NZ) * NXL * NC + (x % NXL) * NC + core % NC
    return ctx * (NZ * NXL * NC) + exp


def moved(array, dy=0, dx=0, dz=0, dcore=0):
    pairs = [
        (linear(y, x, z, c), linear(y + dy, x + dx, z + dz, c + dcore))
        for y in range(NY)
        for x in range(NX)
        for z in range(NZ)
        for c in range(NC)
    ]
    return lax.ppermute(array, AXES, pairs)


def same_core_groups():
    return [[i * NC + c for i in range(CHIPS_EXP)] for c in range(NC)]


def partial_attention(place, q_ref, k_ref, vt_ref, out_ref, s_ref, p_ref):
    source = pl.program_id(0)
    own = place[0]
    rows = q_ref.shape[1]
    keys = k_ref.shape[0]

    def unit(masked):
        stats = []
        for head in range(2):
            query = q_ref[0, :, head * HEAD_DIM : (head + 1) * HEAD_DIM]
            top = jnp.full((8, rows), LOWEST, jnp.float32)
            for start in range(0, keys, KEY_CHUNK):
                part = lax.dot_general(
                    k_ref[start : start + KEY_CHUNK, :],
                    query,
                    (((1,), (1,)), ((), ())),
                    preferred_element_type=jnp.float32,
                )
                if masked:
                    key_at = start + lax.broadcasted_iota(jnp.int32, part.shape, 0)
                    row_at = place[1] + lax.broadcasted_iota(jnp.int32, part.shape, 1)
                    part = jnp.where(key_at <= row_at, part, LOWEST)
                s_ref[head, start : start + KEY_CHUNK, :] = part
                top = jnp.maximum(top, jnp.max(part.reshape(-1, 8, rows), axis=0))
            highest = jnp.max(top, axis=0, keepdims=True) * SCALE2
            total = jnp.zeros((8, rows), jnp.float32)
            for start in range(0, keys, KEY_CHUNK):
                weights = jnp.exp2(s_ref[head, start : start + KEY_CHUNK, :] * SCALE2 - highest)
                total = total + jnp.sum(weights.reshape(-1, 8, rows), axis=0)
                p_ref[head, start : start + KEY_CHUNK, :] = weights.astype(jnp.bfloat16)
            weight_sum = jnp.sum(total, axis=0, keepdims=True)
            mixed = jnp.dot(vt_ref[...], p_ref[head], preferred_element_type=jnp.float32)
            out_ref[0, head * HEAD_DIM : (head + 1) * HEAD_DIM, :] = (mixed / weight_sum).astype(
                jnp.bfloat16
            )
            stats.append(highest + jnp.log2(weight_sum))
        write_stats(stats)

    def write_stats(stats):
        pieces = []
        for stat in stats:
            high = stat.astype(jnp.bfloat16).astype(jnp.float32)
            middle = (stat - high).astype(jnp.bfloat16).astype(jnp.float32)
            pieces += [high, middle, stat - high - middle]
        pieces.append(jnp.zeros((STAT_ROWS - len(pieces), rows), jnp.float32))
        out_ref[0, 2 * HEAD_DIM :, :] = jnp.concatenate(pieces, axis=0).astype(jnp.bfloat16)

    @pl.when(source > own)
    def _():
        unit(False)

    @pl.when(source == own)
    def _():
        unit(True)

    @pl.when(source < own)
    def _():
        out_ref[0, : 2 * HEAD_DIM, :] = jnp.zeros((2 * HEAD_DIM, rows), jnp.bfloat16)
        write_stats([jnp.full((1, rows), LOWEST, jnp.float32)] * 2)


def attend(place, all_queries, keys, values_t):
    sources, rows, width = all_queries.shape
    keys_dev = keys.shape[0]
    out_rows = 2 * HEAD_DIM + STAT_ROWS
    return pl.pallas_call(
        partial_attention,
        out_shape=jax.ShapeDtypeStruct((sources, out_rows, rows), jnp.bfloat16),
        grid_spec=pltpu.PrefetchScalarGridSpec(
            num_scalar_prefetch=1,
            grid=(sources,),
            in_specs=[
                pl.BlockSpec((1, rows, width), lambda i, place: (i, 0, 0)),
                pl.BlockSpec((keys_dev, HEAD_DIM), lambda i, place: (0, 0)),
                pl.BlockSpec((HEAD_DIM, keys_dev), lambda i, place: (0, 0)),
            ],
            out_specs=pl.BlockSpec((1, out_rows, rows), lambda i, place: (i, 0, 0)),
            scratch_shapes=[
                pltpu.VMEM((2, keys_dev, rows), jnp.float32),
                pltpu.VMEM((2, keys_dev, rows), jnp.bfloat16),
            ],
        ),
        compiler_params=pltpu.CompilerParams(vmem_limit_bytes=40 * 1024 * 1024),
    )(place, all_queries, keys, values_t)


def combine(partials):
    shards, _, rows = partials.shape
    mixed = partials[:, : 2 * HEAD_DIM].astype(jnp.float32).reshape(shards, 2, HEAD_DIM, rows)
    stats = partials[:, 2 * HEAD_DIM : 2 * HEAD_DIM + 6].astype(jnp.float32).reshape(shards, 2, 3, rows)
    levels = jnp.sum(stats, axis=2)
    shares = jnp.exp2(levels - jnp.max(levels, axis=0, keepdims=True))
    shares = shares / jnp.sum(shares, axis=0, keepdims=True)
    return jnp.sum(mixed * shares[:, :, None, :], axis=0).astype(jnp.bfloat16).reshape(-1, rows)


def exchange(blocks, axis, groups=None):
    return lax.all_to_all(
        blocks, axis, split_axis=0, concat_axis=0, tiled=True, axis_index_groups=groups
    )


def gather_direct(block, axis):
    return [block] + [moved(block, **{axis: step}) for step in (1, 2, -1)]


def gather_ring(block, axis, size):
    half = size // 2
    pieces = [(0, 0, block)]
    up = down = block
    for step in range(1, half):
        up = moved(up, **{axis: 1})
        down = moved(down, **{axis: -1})
        pieces += [(step, 0, up), (size - step, 0, down)]
    cut = block.shape[0] // 2
    if cut < HALF_ROWS:
        pieces.append((half, 0, moved(up, **{axis: 1})))
    else:
        pieces.append((half, 0, moved(up[:cut], **{axis: 1})))
        pieces.append((half, cut, moved(down[cut:], **{axis: -1})))
    return pieces


def joined(pieces):
    return jnp.concatenate([x for _, _, x in sorted(pieces, key=lambda p: p[:2])], axis=0)


def parted(block, pieces):
    rows = block.shape[0] // (1 + max(r for r, _, _ in pieces))
    return {
        (r, start): block[r * rows + start : r * rows + start + x.shape[0]] for r, start, x in pieces
    }


def add(a, b):
    return (a.astype(jnp.float32) + b.astype(jnp.float32)).astype(jnp.bfloat16)


def reduce_ring(blocks, axis, size):
    half = size // 2
    near, far = blocks[half - 1, 0], blocks[half + 1, 0]
    down = moved(blocks[half, 0], **{axis: -1})
    cut = down.shape[0]
    if cut < near.shape[0]:
        up = moved(blocks[half, cut], **{axis: 1})
        down = jnp.concatenate([add(near[:cut], down), near[cut:]], axis=0)
        up = jnp.concatenate([far[:cut], add(far[cut:], up)], axis=0)
    else:
        down, up = add(near, down), far
    for step in range(half - 2, 0, -1):
        down = add(moved(down, **{axis: -1}), blocks[step, 0])
        up = add(moved(up, **{axis: 1}), blocks[size - step, 0])
    down = moved(down, **{axis: -1})
    up = moved(up, **{axis: 1})
    return (
        blocks[0, 0].astype(jnp.float32) + down.astype(jnp.float32) + up.astype(jnp.float32)
    ).astype(jnp.bfloat16)


def reduce_direct(block, axis):
    own, near, across, far = jnp.split(block, 4, axis=0)
    terms = [
        own,
        moved(near, **{axis: -1}),
        moved(far, **{axis: 1}),
        moved(across, **{axis: -2}),
    ]
    return sum(t.astype(jnp.float32) for t in terms)


def experts_body(spans_a, spans_b, line_rows, expert_ids, *refs):
    refs = list(refs)

    def take(count):
        taken = refs[:count]
        del refs[:count]
        return taken

    in_a, in_b = take(len(spans_a)), take(len(spans_b))
    own_in, other_in, own_down, other_down = take(4)
    out_a, out_b = take(len(spans_a)), take(len(spans_b))
    tokens, gates, acts = refs
    local_experts = own_in.shape[0]
    hidden = own_in.shape[2] // 2
    plane_rows = NY * line_rows
    total_rows = NZ * plane_rows

    def lines_b(r, start, rows):
        return [
            (z * line_rows - start, z * plane_rows + r * line_rows)
            for z in range(start // line_rows, (start + rows) // line_rows)
        ]

    for (r, start, rows), x_ref in zip(spans_a, in_a):
        at = r * plane_rows + start
        tokens[at : at + rows, :COLS_A] = x_ref[:, :COLS_A]
        gates[at : at + rows, :] = x_ref[:, COLS_A:]
    for span, x_ref in zip(spans_b, in_b):
        for here, at in lines_b(*span):
            tokens[at : at + line_rows, COLS_A:] = x_ref[here : here + line_rows, :]

    def f32dot(x, y):
        return jnp.dot(x, y, preferred_element_type=jnp.float32)

    for e in range(2 * local_experts):
        w_ref = (own_in if e < local_experts else other_in).at[e % local_experts]
        pick = (
            lax.broadcasted_iota(jnp.int32, (GATE_COLS, hidden), 0) % (GATE_COLS // 2)
            == expert_ids[e]
        ).astype(jnp.bfloat16)
        for at in range(0, total_rows, UP_ROWS):
            rows = slice(at, at + UP_ROWS)
            both = f32dot(tokens[rows, :], w_ref[...])
            factor = f32dot(gates[rows, :], pick)
            gate, up = both[:, :hidden], both[:, hidden:]
            act = gate / (1.0 + jnp.exp(-gate)) * up * factor
            acts[rows, e * hidden : (e + 1) * hidden] = act.astype(jnp.bfloat16)

    split = local_experts * hidden
    places_a = {
        r * plane_rows + start + extra: (y_ref, extra)
        for (r, start, rows), y_ref in zip(spans_a, out_a)
        for extra in range(0, rows, line_rows)
    }
    places_b = {
        at: (y_ref, here) for span, y_ref in zip(spans_b, out_b) for here, at in lines_b(*span)
    }
    for at in range(0, total_rows, DOWN_ROWS):
        act = acts[at : at + DOWN_ROWS, :]
        for places, first, last in (
            (places_a, 0, COLS_A),
            (places_b, COLS_A, tokens.shape[1]),
        ):
            for column in range(first, last, DOWN_COLS):
                columns = slice(column, column + DOWN_COLS)
                y = f32dot(act[:, :split], own_down[:, columns]) + f32dot(
                    act[:, split:], other_down[:, columns]
                )
                y = y.astype(jnp.bfloat16)
                for line in range(0, DOWN_ROWS, line_rows):
                    y_ref, here = places[at + line]
                    y_ref[here : here + line_rows, column - first : column - first + DOWN_COLS] = y[
                        line : line + line_rows
                    ]


def run_experts(expert_ids, pieces_a, pieces_b, line_rows, own_in, other_in, own_down, other_down):
    spans_a = [(r, start, x.shape[0]) for r, start, x in pieces_a]
    spans_b = [(r, start, x.shape[0]) for r, start, x in pieces_b]
    cols_b = pieces_b[0][2].shape[1]
    rows = NY * NZ * line_rows
    local_experts, _, width = own_in.shape
    hidden = width // 2
    whole = pl.BlockSpec(memory_space=pltpu.VMEM)
    operands = [x for _, _, x in pieces_a + pieces_b] + [own_in, other_in, own_down, other_down]
    results = pl.pallas_call(
        functools.partial(experts_body, spans_a, spans_b, line_rows),
        out_shape=[jax.ShapeDtypeStruct((n, COLS_A), jnp.bfloat16) for _, _, n in spans_a]
        + [jax.ShapeDtypeStruct((n, cols_b), jnp.bfloat16) for _, _, n in spans_b],
        in_specs=[pl.BlockSpec(memory_space=pltpu.SMEM)] + [whole] * len(operands),
        out_specs=[whole] * (len(spans_a) + len(spans_b)),
        scratch_shapes=[
            pltpu.VMEM((rows, COLS_A + cols_b), jnp.bfloat16),
            pltpu.VMEM((rows, GATE_COLS), jnp.bfloat16),
            pltpu.VMEM((rows, 2 * local_experts * hidden), jnp.bfloat16),
        ],
        compiler_params=pltpu.CompilerParams(vmem_limit_bytes=VMEM_LIMIT),
    )(expert_ids, *operands)
    terms_a = {(r, start): y for (r, start, _), y in zip(spans_a, results)}
    terms_b = {(r, start): y for (r, start, _), y in zip(spans_b, results[len(spans_a) :])}
    return terms_a, terms_b


def gate_columns(ids, weights, experts):
    matches = ids[:, :, None] == jnp.arange(experts, dtype=jnp.int32)[None, None, :]
    dense = jnp.sum(jnp.where(matches, weights[:, :, None], 0.0), axis=1)
    high = dense.astype(jnp.bfloat16)
    low = (dense - high.astype(jnp.float32)).astype(jnp.bfloat16)
    return jnp.concatenate([high, low], axis=1)


def on_device(
    queries,
    keys,
    values,
    block_offsets,
    w_out,
    residual,
    norm_gain,
    expert_ids,
    gate_weights,
    w_gate,
    w_up,
    w_down,
):
    ctx_pos = lax.axis_index("ctx")
    exp_pos = lax.axis_index("exp")
    core = exp_pos % NC
    block_len, query_width = queries.shape
    model_width = residual.shape[1]
    half_width = model_width // 2
    heads_here = query_width // HEAD_DIM
    key_head = exp_pos * heads_here // (Q_HEADS // KV_HEADS)

    local_experts, _, hidden = w_gate.shape
    experts = local_experts * lax.axis_size("exp")
    own_in = jnp.concatenate([w_gate, w_up], axis=2)
    own_down = w_down.reshape(local_experts * hidden, model_width)
    own_out = lax.dynamic_slice_in_dim(w_out, core * half_width, half_width, 1)
    give_out = lax.dynamic_slice_in_dim(w_out, (1 - core) * half_width, half_width, 1)
    other_out = moved(give_out, dcore=1)
    other_down = moved(own_down, dcore=1)

    place = jnp.stack([ctx_pos, block_offsets[ctx_pos]]).astype(jnp.int32)
    head_keys = lax.dynamic_slice_in_dim(keys, key_head * HEAD_DIM, HEAD_DIM, 1)
    head_values = lax.dynamic_slice_in_dim(values, key_head * HEAD_DIM, HEAD_DIM, 1).T
    copies = lax.optimization_barrier(
        jnp.broadcast_to(queries[None], (CTX, block_len, query_width))
    )
    all_queries, own_in = lax.optimization_barrier((exchange(copies, "ctx"), own_in))
    other_in = moved(own_in, dcore=1)
    partials = attend(place, all_queries, head_keys, head_values)
    own_att = combine(exchange(partials, "ctx"))
    own_att, own_out, other_out, other_in, other_down = lax.optimization_barrier(
        (own_att, own_out, other_out, other_in, other_down)
    )
    other_att = moved(own_att, dcore=1)

    contract = (((0,), (0,)), ((), ()))
    projected = lax.dot_general(
        own_att, own_out, contract, preferred_element_type=jnp.float32
    ) + lax.dot_general(other_att, other_out, contract, preferred_element_type=jnp.float32)
    chip_rows = block_len // CHIPS_EXP
    rows_dev = chip_rows // NC
    terms = projected.astype(jnp.bfloat16).reshape(CHIPS_EXP, chip_rows, half_width)
    terms = exchange(terms, "exp", same_core_groups())
    att_half = jnp.sum(terms.astype(jnp.float32), axis=0).astype(jnp.bfloat16)
    keep = lax.dynamic_slice_in_dim(att_half, core * rows_dev, rows_dev, 0)
    give = lax.dynamic_slice_in_dim(att_half, (1 - core) * rows_dev, rows_dev, 0)
    came = moved(give, dcore=1)
    attended = jnp.where(
        core == 0,
        jnp.concatenate([keep, came], axis=1),
        jnp.concatenate([came, keep], axis=1),
    )

    hidden_rows = residual.astype(jnp.float32) + attended.astype(jnp.float32)
    normed = (
        hidden_rows
        * lax.rsqrt(jnp.mean(hidden_rows * hidden_rows, axis=1, keepdims=True) + 1e-06)
        * norm_gain
    ).astype(jnp.bfloat16)

    gates = gate_columns(expert_ids[ctx_pos], gate_weights[ctx_pos], experts)
    row = jnp.concatenate([normed[:, :COLS_A], gates, normed[:, COLS_A:]], axis=1)
    line_a = jnp.concatenate(gather_direct(row[:, :SPLIT], "dx"), axis=0)
    sheet_a = jnp.concatenate(gather_direct(line_a, "dy"), axis=0)
    pieces_a = gather_ring(sheet_a, "dz", NZ)
    found_z = gather_ring(row[:, SPLIT:], "dz", NZ)
    found_x = gather_ring(joined(found_z), "dx", NX)
    cols_b = row.shape[1] - SPLIT
    sheet_b = joined(found_x).reshape(NX, NZ, rows_dev, cols_b).transpose(1, 0, 2, 3)
    pieces_b = gather_ring(sheet_b.reshape(-1, cols_b), "dy", NY)
    line_rows = NX * rows_dev

    chip_first = (exp_pos - core) * local_experts
    chip_experts = [
        chip_first + side * local_experts + local
        for side in (core, 1 - core)
        for local in range(local_experts)
    ]
    terms_a, terms_b = run_experts(
        jnp.stack(chip_experts).astype(jnp.int32),
        pieces_a,
        pieces_b,
        line_rows,
        own_in,
        other_in,
        own_down,
        other_down,
    )

    sum_a = reduce_ring(terms_a, "dz", NZ)
    sum_b = reduce_ring(terms_b, "dy", NY)
    line_a = reduce_direct(sum_a, "dy").astype(jnp.bfloat16)
    own_a = reduce_direct(line_a, "dx").astype(jnp.bfloat16)
    sum_b = sum_b.reshape(NZ, NX, rows_dev, cols_b).transpose(1, 0, 2, 3).reshape(-1, cols_b)
    sum_b = reduce_ring(parted(sum_b, found_x), "dx", NX)
    own_b = reduce_ring(parted(sum_b, found_z), "dz", NZ)
    return (attended, jnp.concatenate([own_a, own_b], axis=1))


def solution(mesh):
    in_specs = (
        P("ctx", "exp"),
        P("ctx", None),
        P("ctx", None),
        P(),
        P("exp", None),
        P(("ctx", "exp"), None),
        P(),
        P(None, "exp", None),
        P(None, "exp", None),
        P("exp", None, "ctx"),
        P("exp", None, "ctx"),
        P("exp", "ctx", None),
    )
    out_specs = (P(("ctx", "exp"), None), P(("ctx", "exp"), None))
    return jax.shard_map(
        on_device, mesh=mesh, in_specs=in_specs, out_specs=out_specs, check_vma=False
    )
```

```python
import functools
import math

import jax
import jax.numpy as jnp
from jax import lax
from jax.experimental import pallas as pl
from jax.experimental.pallas import tpu as pltpu
from jax.sharding import PartitionSpec as P

Q_HEADS = 64
KV_HEADS = 4
HEAD_DIM = 128

NY, NXH, NZ, NXL, NC = 4, 2, 8, 2, 2
NX = NXH * NXL
CTX = NY * NXH
CHIPS_EXP = NZ * NXL
AXES = ("ctx", "exp")

LOWEST = -1e30
SCALE = 1.0 / math.sqrt(HEAD_DIM)
SCALE2 = SCALE * math.log2(math.e)

COLS_A = 2048
GATE_COLS = 128
SPLIT = COLS_A + GATE_COLS

STAT_ROWS = 16
KEY_CHUNK = 256
VMEM_LIMIT = 56 * 1024 * 1024
UP_ROWS = 512
DOWN_COLS = 256


def linear(y, x, z, core):
    ctx = (y % NY) * NXH + (x % NX) // NXL
    exp = (z % NZ) * NXL * NC + (x % NXL) * NC + core % NC
    return ctx * (NZ * NXL * NC) + exp


def moved(array, dy=0, dx=0, dz=0, dcore=0):
    pairs = [
        (linear(y, x, z, c), linear(y + dy, x + dx, z + dz, c + dcore))
        for y in range(NY)
        for x in range(NX)
        for z in range(NZ)
        for c in range(NC)
    ]
    return lax.ppermute(array, AXES, pairs)


def z_groups():
    rest = NXL * NC
    return [[z * rest + i for z in range(NZ)] for i in range(rest)]


def same_core_groups():
    return [[i * NC + c for i in range(CHIPS_EXP)] for c in range(NC)]


def partial_attention(place, q_ref, k_ref, vt_ref, out_ref, s_ref, p_ref):
    source = pl.program_id(0)
    own = place[0]
    rows = q_ref.shape[1]
    keys = k_ref.shape[0]

    def unit(masked):
        stats = []
        for head in range(2):
            query = q_ref[0, :, head * HEAD_DIM : (head + 1) * HEAD_DIM]
            top = jnp.full((8, rows), LOWEST, jnp.float32)
            for start in range(0, keys, KEY_CHUNK):
                part = lax.dot_general(
                    k_ref[start : start + KEY_CHUNK, :],
                    query,
                    (((1,), (1,)), ((), ())),
                    preferred_element_type=jnp.float32,
                )
                if masked:
                    key_at = start + lax.broadcasted_iota(jnp.int32, part.shape, 0)
                    row_at = place[1] + lax.broadcasted_iota(jnp.int32, part.shape, 1)
                    part = jnp.where(key_at <= row_at, part, LOWEST)
                s_ref[head, start : start + KEY_CHUNK, :] = part
                top = jnp.maximum(top, jnp.max(part.reshape(-1, 8, rows), axis=0))
            highest = jnp.max(top, axis=0, keepdims=True) * SCALE2
            total = jnp.zeros((8, rows), jnp.float32)
            for start in range(0, keys, KEY_CHUNK):
                weights = jnp.exp2(s_ref[head, start : start + KEY_CHUNK, :] * SCALE2 - highest)
                total = total + jnp.sum(weights.reshape(-1, 8, rows), axis=0)
                p_ref[head, start : start + KEY_CHUNK, :] = weights.astype(jnp.bfloat16)
            weight_sum = jnp.sum(total, axis=0, keepdims=True)
            mixed = jnp.dot(vt_ref[...], p_ref[head], preferred_element_type=jnp.float32)
            out_ref[0, head * HEAD_DIM : (head + 1) * HEAD_DIM, :] = (mixed / weight_sum).astype(
                jnp.bfloat16
            )
            stats.append(highest + jnp.log2(weight_sum))
        write_stats(stats)

    def write_stats(stats):
        pieces = []
        for stat in stats:
            high = stat.astype(jnp.bfloat16).astype(jnp.float32)
            middle = (stat - high).astype(jnp.bfloat16).astype(jnp.float32)
            pieces += [high, middle, stat - high - middle]
        pieces.append(jnp.zeros((STAT_ROWS - len(pieces), rows), jnp.float32))
        out_ref[0, 2 * HEAD_DIM :, :] = jnp.concatenate(pieces, axis=0).astype(jnp.bfloat16)

    @pl.when(source > own)
    def _():
        unit(False)

    @pl.when(source == own)
    def _():
        unit(True)

    @pl.when(source < own)
    def _():
        out_ref[0, : 2 * HEAD_DIM, :] = jnp.zeros((2 * HEAD_DIM, rows), jnp.bfloat16)
        write_stats([jnp.full((1, rows), LOWEST, jnp.float32)] * 2)


def attend(place, all_queries, keys, values_t):
    sources, rows, width = all_queries.shape
    keys_dev = keys.shape[0]
    out_rows = 2 * HEAD_DIM + STAT_ROWS
    return pl.pallas_call(
        partial_attention,
        out_shape=jax.ShapeDtypeStruct((sources, out_rows, rows), jnp.bfloat16),
        grid_spec=pltpu.PrefetchScalarGridSpec(
            num_scalar_prefetch=1,
            grid=(sources,),
            in_specs=[
                pl.BlockSpec((1, rows, width), lambda i, place: (i, 0, 0)),
                pl.BlockSpec((keys_dev, HEAD_DIM), lambda i, place: (0, 0)),
                pl.BlockSpec((HEAD_DIM, keys_dev), lambda i, place: (0, 0)),
            ],
            out_specs=pl.BlockSpec((1, out_rows, rows), lambda i, place: (i, 0, 0)),
            scratch_shapes=[
                pltpu.VMEM((2, keys_dev, rows), jnp.float32),
                pltpu.VMEM((2, keys_dev, rows), jnp.bfloat16),
            ],
        ),
        compiler_params=pltpu.CompilerParams(vmem_limit_bytes=40 * 1024 * 1024),
    )(place, all_queries, keys, values_t)


def combine(partials):
    shards, _, rows = partials.shape
    mixed = partials[:, : 2 * HEAD_DIM].astype(jnp.float32).reshape(shards, 2, HEAD_DIM, rows)
    stats = partials[:, 2 * HEAD_DIM : 2 * HEAD_DIM + 6].astype(jnp.float32).reshape(shards, 2, 3, rows)
    levels = jnp.sum(stats, axis=2)
    shares = jnp.exp2(levels - jnp.max(levels, axis=0, keepdims=True))
    shares = shares / jnp.sum(shares, axis=0, keepdims=True)
    return jnp.sum(mixed * shares[:, :, None, :], axis=0).astype(jnp.bfloat16).reshape(-1, rows)


def exchange(blocks, axis, groups=None):
    return lax.all_to_all(
        blocks, axis, split_axis=0, concat_axis=0, tiled=True, axis_index_groups=groups
    )


def gather_direct(block, axis):
    return [block] + [moved(block, **{axis: step}) for step in (1, 2, -1)]


def both_ways(up, down, axis):
    return moved(up, **{axis: 1}), moved(down, **{axis: -1})


def together(*arrays):
    return lax.optimization_barrier(arrays)


def gather_rings(sheet_a, sheet_b):
    cut = sheet_a.shape[0] // 2
    up_a, down_a = both_ways(sheet_a, sheet_a, "dy")
    up_b, down_b = both_ways(sheet_b, sheet_b, "dx")
    up_a, down_a, up_b, down_b = together(up_a, down_a, up_b, down_b)
    far_a = both_ways(up_a[:cut], down_a[cut:], "dy")
    far_b = both_ways(up_b[:cut], down_b[cut:], "dx")
    return [
        [(0, 0, sheet), (1, 0, up), (3, 0, down), (2, 0, far[0]), (2, cut, far[1])]
        for sheet, up, down, far in ((sheet_a, up_a, down_a, far_a), (sheet_b, up_b, down_b, far_b))
    ]


def add(*terms):
    return sum(t.astype(jnp.float32) for t in terms).astype(jnp.bfloat16)


def extended(block, before, after):
    return lax.pad(block, jnp.zeros((), block.dtype), ((before, after, 0), (0, 0, 0)))


def reduce_rings(terms_a, terms_b):
    cut = terms_a[2, 0].shape[0]
    up_a, down_a = both_ways(terms_a[2, cut], terms_a[2, 0], "dy")
    up_b, down_b = both_ways(terms_b[2, cut], terms_b[2, 0], "dx")
    up_a, down_a, up_b, down_b = together(up_a, down_a, up_b, down_b)
    up_a = add(terms_a[3, 0], extended(up_a, cut, 0))
    down_a = add(terms_a[1, 0], extended(down_a, 0, cut))
    up_b = add(terms_b[3, 0], extended(up_b, cut, 0))
    down_b = add(terms_b[1, 0], extended(down_b, 0, cut))
    up_a, down_a, up_b, down_b = together(up_a, down_a, up_b, down_b)
    up_a, down_a = both_ways(up_a, down_a, "dy")
    up_b, down_b = both_ways(up_b, down_b, "dx")
    up_a, down_a, up_b, down_b = together(up_a, down_a, up_b, down_b)
    return add(terms_a[0, 0], up_a, down_a), add(terms_b[0, 0], up_b, down_b)


def reduce_direct(block, axis):
    own, near, across, far = jnp.split(block, 4, axis=0)
    terms = [
        own,
        moved(near, **{axis: -1}),
        moved(far, **{axis: 1}),
        moved(across, **{axis: -2}),
    ]
    return add(*terms)


def lines_b(span, line_rows):
    r, start, rows = span
    return [
        (y * line_rows - start, (y * NX + r) * line_rows)
        for y in range(start // line_rows, (start + rows) // line_rows)
    ]


def f32dot(x, y):
    return jnp.dot(x, y, preferred_element_type=jnp.float32)


def write_terms(acts, own_down, other_down, spans_a, out_a, spans_b, out_b, line_rows):
    split = own_down.shape[0]
    plane_rows = NX * line_rows

    def down(act, first, last):
        for column in range(first, last, DOWN_COLS):
            columns = slice(column, column + DOWN_COLS)
            y = f32dot(act[:, :split], own_down[:, columns])
            y = y + f32dot(act[:, split:], other_down[:, columns])
            yield slice(column - first, column - first + DOWN_COLS), y.astype(jnp.bfloat16)

    firsts = [r * plane_rows + start for r, start, _ in spans_a]
    begin = 0
    while begin < len(spans_a):
        end = begin + 1
        while end < len(spans_a) and firsts[end] == firsts[end - 1] + spans_a[end - 1][2]:
            end += 1
        low, high = firsts[begin], firsts[end - 1] + spans_a[end - 1][2]
        for columns, y in down(acts[low:high, :], 0, COLS_A):
            for i in range(begin, end):
                at = firsts[i] - low
                out_a[i][:, columns] = y[at : at + spans_a[i][2]]
        begin = end
    for span, y_ref in zip(spans_b, out_b):
        rows = [acts[at : at + line_rows, :] for _, at in lines_b(span, line_rows)]
        act = jnp.concatenate(rows, axis=0)
        for columns, y in down(act, COLS_A, own_down.shape[1]):
            y_ref[:, columns] = y


def taker(refs):
    refs = list(refs)

    def take(count):
        taken = refs[:count]
        del refs[:count]
        return taken

    return take


def experts_body(spans_a, spans_b, early_a, early_b, line_rows, expert_ids, *refs):
    take = taker(refs)
    in_a, in_b = take(len(spans_a)), take(len(spans_b))
    own_in, other_in, own_down, other_down = take(4)
    out_a, out_b = take(len(early_a)), take(len(early_b))
    acts, tokens, gates = take(3)
    local_experts = own_in.shape[0]
    hidden = own_in.shape[2] // 2
    plane_rows = NX * line_rows

    for (r, start, rows), x_ref in zip(spans_a, in_a):
        at = r * plane_rows + start
        tokens[at : at + rows, :COLS_A] = x_ref[:, :COLS_A]
        gates[at : at + rows, :] = x_ref[:, COLS_A:]
    for span, x_ref in zip(spans_b, in_b):
        for here, at in lines_b(span, line_rows):
            tokens[at : at + line_rows, COLS_A:] = x_ref[here : here + line_rows, :]

    for e in range(2 * local_experts):
        w_ref = (own_in if e < local_experts else other_in).at[e % local_experts]
        pick = (
            lax.broadcasted_iota(jnp.int32, (GATE_COLS, hidden), 0) % (GATE_COLS // 2)
            == expert_ids[e]
        ).astype(jnp.bfloat16)
        for at in range(0, NY * plane_rows, UP_ROWS):
            rows = slice(at, at + UP_ROWS)
            both = f32dot(tokens[rows, :], w_ref[...])
            factor = f32dot(gates[rows, :], pick)
            gate, up = both[:, :hidden], both[:, hidden:]
            act = gate / (1.0 + jnp.exp(-gate)) * up * factor
            acts[rows, e * hidden : (e + 1) * hidden] = act.astype(jnp.bfloat16)

    write_terms(acts, own_down, other_down, early_a, out_a, early_b, out_b, line_rows)


def down_body(late_a, late_b, line_rows, acts, own_down, other_down, *refs):
    take = taker(refs)
    out_a, out_b = take(len(late_a)), take(len(late_b))
    write_terms(acts, own_down, other_down, late_a, out_a, late_b, out_b, line_rows)


def run_experts(expert_ids, pieces_a, pieces_b, line_rows, own_in, other_in, own_down, other_down):
    spans_a = [(r, start, x.shape[0]) for r, start, x in pieces_a]
    spans_b = [(r, start, x.shape[0]) for r, start, x in pieces_b]
    cols_b = pieces_b[0][2].shape[1]
    rows = NX * NY * line_rows
    local_experts, _, width = own_in.shape
    hidden_all = local_experts * width
    whole = pl.BlockSpec(memory_space=pltpu.VMEM)
    early_a = sorted(x for x in spans_a if x[0] == NY // 2)
    early_b = sorted(x for x in spans_b if x[0] == NX // 2)
    late_a = sorted(x for x in spans_a if x not in early_a)
    late_b = sorted(x for x in spans_b if x not in early_b)

    def outputs(a, b):
        return [jax.ShapeDtypeStruct((x[2], COLS_A), jnp.bfloat16) for x in a] + [
            jax.ShapeDtypeStruct((x[2], cols_b), jnp.bfloat16) for x in b
        ]

    operands = [x for _, _, x in pieces_a + pieces_b] + [own_in, other_in, own_down, other_down]
    early = pl.pallas_call(
        functools.partial(experts_body, spans_a, spans_b, early_a, early_b, line_rows),
        out_shape=outputs(early_a, early_b) + [jax.ShapeDtypeStruct((rows, hidden_all), jnp.bfloat16)],
        in_specs=[pl.BlockSpec(memory_space=pltpu.SMEM)] + [whole] * len(operands),
        out_specs=[whole] * (len(early_a) + len(early_b) + 1),
        scratch_shapes=[
            pltpu.VMEM((rows, COLS_A + cols_b), jnp.bfloat16),
            pltpu.VMEM((rows, GATE_COLS), jnp.bfloat16),
        ],
        compiler_params=pltpu.CompilerParams(vmem_limit_bytes=VMEM_LIMIT),
    )(expert_ids, *operands)
    late = pl.pallas_call(
        functools.partial(down_body, late_a, late_b, line_rows),
        out_shape=outputs(late_a, late_b),
        in_specs=[whole] * 3,
        out_specs=[whole] * (len(late_a) + len(late_b)),
        compiler_params=pltpu.CompilerParams(vmem_limit_bytes=VMEM_LIMIT),
    )(early[-1], own_down, other_down)
    terms_a = dict(zip([x[:2] for x in early_a + late_a], early[: len(early_a)] + late[: len(late_a)]))
    terms_b = dict(zip([x[:2] for x in early_b + late_b], early[len(early_a) : -1] + late[len(late_a) :]))
    return terms_a, terms_b


def gate_columns(ids, weights, experts):
    matches = ids[:, :, None] == jnp.arange(experts, dtype=jnp.int32)[None, None, :]
    dense = jnp.sum(jnp.where(matches, weights[:, :, None], 0.0), axis=1)
    high = dense.astype(jnp.bfloat16)
    low = (dense - high.astype(jnp.float32)).astype(jnp.bfloat16)
    return jnp.concatenate([high, low], axis=1)


def on_device(
    queries,
    keys,
    values,
    block_offsets,
    w_out,
    residual,
    norm_gain,
    expert_ids,
    gate_weights,
    w_gate,
    w_up,
    w_down,
):
    ctx_pos = lax.axis_index("ctx")
    exp_pos = lax.axis_index("exp")
    core = exp_pos % NC
    block_len, query_width = queries.shape
    model_width = residual.shape[1]
    half_width = model_width // 2
    heads_here = query_width // HEAD_DIM
    key_head = exp_pos * heads_here // (Q_HEADS // KV_HEADS)

    local_experts, _, hidden = w_gate.shape
    experts = local_experts * lax.axis_size("exp")
    own_in = jnp.concatenate([w_gate, w_up], axis=2)
    own_down = w_down.reshape(local_experts * hidden, model_width)
    own_out = lax.dynamic_slice_in_dim(w_out, core * half_width, half_width, 1)
    give_out = lax.dynamic_slice_in_dim(w_out, (1 - core) * half_width, half_width, 1)
    other_out = moved(give_out, dcore=1)
    other_down = moved(own_down, dcore=1)

    chip_first = (exp_pos - core) * local_experts
    chip_experts = [
        chip_first + side * local_experts + local
        for side in (core, 1 - core)
        for local in range(local_experts)
    ]
    chip_experts = jnp.stack(chip_experts).astype(jnp.int32)

    place = jnp.stack([ctx_pos, block_offsets[ctx_pos]]).astype(jnp.int32)
    head_keys = lax.dynamic_slice_in_dim(keys, key_head * HEAD_DIM, HEAD_DIM, 1)
    head_values = lax.dynamic_slice_in_dim(values, key_head * HEAD_DIM, HEAD_DIM, 1).T
    copies = lax.optimization_barrier(
        jnp.broadcast_to(queries[None], (CTX, block_len, query_width))
    )
    all_queries, own_in, head_keys, head_values, place = lax.optimization_barrier(
        (exchange(copies, "ctx"), own_in, head_keys, head_values, place)
    )
    other_in = moved(own_in, dcore=1)
    partials = attend(place, all_queries, head_keys, head_values)
    own_att = combine(exchange(partials, "ctx"))
    own_att, own_out, other_out, other_in, other_down, chip_experts = together(
        own_att, own_out, other_out, other_in, other_down, chip_experts
    )
    other_att = moved(own_att, dcore=1)

    contract = (((0,), (0,)), ((), ()))
    projected = lax.dot_general(
        own_att, own_out, contract, preferred_element_type=jnp.float32
    ) + lax.dot_general(other_att, other_out, contract, preferred_element_type=jnp.float32)
    chip_rows = block_len // CHIPS_EXP
    rows_dev = chip_rows // NC
    terms = projected.astype(jnp.bfloat16).reshape(CHIPS_EXP, chip_rows, half_width)
    terms = exchange(terms, "exp", same_core_groups())
    att_half = jnp.sum(terms.astype(jnp.float32), axis=0).astype(jnp.bfloat16)
    keep = lax.dynamic_slice_in_dim(att_half, core * rows_dev, rows_dev, 0)
    give = lax.dynamic_slice_in_dim(att_half, (1 - core) * rows_dev, rows_dev, 0)
    came = moved(give, dcore=1)
    attended = jnp.where(
        core == 0,
        jnp.concatenate([keep, came], axis=1),
        jnp.concatenate([came, keep], axis=1),
    )

    hidden_rows = residual.astype(jnp.float32) + attended.astype(jnp.float32)
    normed = (
        hidden_rows
        * lax.rsqrt(jnp.mean(hidden_rows * hidden_rows, axis=1, keepdims=True) + 1e-06)
        * norm_gain
    ).astype(jnp.bfloat16)

    gates = gate_columns(expert_ids[ctx_pos], gate_weights[ctx_pos], experts)
    row = jnp.concatenate([normed[:, :COLS_A], gates, normed[:, COLS_A:]], axis=1)
    copies = lax.optimization_barrier(jnp.broadcast_to(row[None], (NZ,) + row.shape))
    lines = exchange(copies, "exp", z_groups()).reshape(-1, row.shape[1])
    line_rows = lines.shape[0]
    sheet_a = jnp.concatenate(gather_direct(lines[:, :SPLIT], "dx"), axis=0)
    sheet_b = jnp.concatenate(gather_direct(lines[:, SPLIT:], "dy"), axis=0)
    sheet_a, sheet_b = together(sheet_a, sheet_b)
    pieces_a, pieces_b = gather_rings(sheet_a, sheet_b)

    terms_a, terms_b = run_experts(
        chip_experts,
        pieces_a,
        pieces_b,
        line_rows,
        own_in,
        other_in,
        own_down,
        other_down,
    )

    sum_a, sum_b = reduce_rings(terms_a, terms_b)
    lines = jnp.concatenate([reduce_direct(sum_a, "dx"), reduce_direct(sum_b, "dy")], axis=1)
    terms = exchange(lines.reshape(NZ, rows_dev, model_width), "exp", z_groups())
    mixture = jnp.sum(terms.astype(jnp.float32), axis=0).astype(jnp.bfloat16)
    return (attended, mixture)


def solution(mesh):
    in_specs = (
        P("ctx", "exp"),
        P("ctx", None),
        P("ctx", None),
        P(),
        P("exp", None),
        P(("ctx", "exp"), None),
        P(),
        P(None, "exp", None),
        P(None, "exp", None),
        P("exp", None, "ctx"),
        P("exp", None, "ctx"),
        P("exp", "ctx", None),
    )
    out_specs = (P(("ctx", "exp"), None), P(("ctx", "exp"), None))
    return jax.shard_map(
        on_device, mesh=mesh, in_specs=in_specs, out_specs=out_specs, check_vma=False
    )
```
